32 devices in a mesh: expert: 8 (over z, core), shard: 4 (over y, x).
Axes of the slice: x: 2, y: 2, z: 4, core: 2. Of those that a mesh axis runs over, the one named last changes fastest.
Arguments:
- tokens: bfloat16 [8192, 768], P(('expert', 'shard')), may hold values from -6 to 6
- segments: int32 [8192], P(('expert', 'shard')), may hold values from 0 to 2, as said below
- routes: int32 [8192, 1], P(('expert', 'shard')), may hold values from 0 to 7; in each aligned block of 256 rows (0 to 255, 256 to 511, ...) at most 64 rows name the same one
- buckets: int32 [2047], replicated, may hold values from 0 to 31
- gain_attn: float32 [768], replicated, may hold values from 0.5 to 1.5
- gain_moe: float32 [768], replicated, may hold values from 0.5 to 1.5
- rel_table: float32 [32, 12], replicated, may hold values from -6 to 6
- router_weight: float32 [768, 8], replicated, may hold values from -0.111 to 0.111
- qkv_weight: bfloat16 [768, 2304], P('shard'), may hold values from -0.21875 to 0.21875
- out_weight: bfloat16 [768, 768], P('shard'), may hold values from -3.5 to 3.5
- w_in: bfloat16 [8, 768, 3072], P('expert', 'shard'), may hold values from -0.21875 to 0.21875
- w_out: bfloat16 [8, 3072, 768], P('expert', 'shard'), may hold values from -0.875 to 0.875
- out_grad: bfloat16 [8192, 768], P(('expert', 'shard')), may hold values from -6 to 6
Outputs:
- output: bfloat16 [8192, 768], P(('expert', 'shard'))
- grad_tokens: float32 [8192, 768], P(('expert', 'shard'))
- grad_gain_attn: float32 [768], replicated
- grad_gain_moe: float32 [768], replicated
- grad_rel_table: float32 [32, 12], replicated
- grad_router: float32 [768, 8], replicated
- grad_qkv_weight: float32 [768, 2304], P('shard')
- grad_out_weight: float32 [768, 768], P('shard')
- grad_w_in: float32 [8, 768, 3072], P('expert', 'shard')
- grad_w_out: float32 [8, 3072, 768], P('expert', 'shard')
The draws below stay inside these ranges and needn't reach their ends.
Inputs may be any that keep to these rules, and one draw needn't show every extreme that they name: `segments`: within each sequence of 1024 tokens the numbers are 0, 1, 2 in order, each present; number 1 begins within the sequence's first 256 tokens and number 2 within its last 256. `routes`: in each aligned block of 256 rows (the rows of one device) no expert is named by more than 64 rows, a bound that some block reaches.
All inputs are finite; a program needn't handle non-finite values.
Results may differ from the reference program's by a relative error of at most 0.03.
Values may be sent and summed in bfloat16 or wider, within the bound.
A program may use at most 192 MiB of HBM per device.

```python
import math
import jax
import jax.numpy as jnp
import numpy as np
from jax import lax

D = 768
H = 12
HD = 64
FF = 3072
NB = 32
TOK_DEV = 256
EXPERTS = 8
LEN = 1024
SEQS = 8
TOKENS = 8192
CAP = 64


def draw_segments(key, part):
    key = jax.random.fold_in(key, 7)
    first_key, second_key = jax.random.split(key)
    opening = jax.random.randint(first_key, (SEQS, 1), 1, TOK_DEV)
    closing = jax.random.randint(second_key, (SEQS, 1), 1, TOK_DEV)
    position_grid = jnp.arange(LEN, dtype=jnp.int32)[None, :]
    numbers = (position_grid >= opening).astype(jnp.int32) + (position_grid >= LEN - closing).astype(jnp.int32)
    return numbers.reshape(-1).astype(jnp.int32)


def place_ends(drawn, rng, least, largest):
    dims = drawn.shape
    spot = [jax.random.randint(jax.random.fold_in(rng, axis), (), 0, dims[axis]) for axis in range(len(dims))]
    drawn = drawn.at[tuple(spot)].set(least)
    longest = dims.index(max(dims))
    spot[longest] = (spot[longest] + 1) % dims[longest]
    return drawn.at[tuple(spot)].set(largest)


def steps_of(rng, shape, shards, smallest, top_value):
    level, own = 1.0, jax.random.fold_in(rng, 6)
    for axis_at, blocks in shards:
        steps = jnp.exp(jax.random.uniform(jax.random.fold_in(own, axis_at), (blocks,), jnp.float32, smallest / len(shards), top_value / len(shards)))
        level = level * jnp.repeat(steps, shape[axis_at] // blocks).reshape([-1 if axis == axis_at else 1 for axis in range(len(shape))])
    return level


def assign_block(rng, own, number, rows, number_of, top, reach, slope):
    order = jax.random.permutation(rng, number_of)
    packed, usual = portions_of(number_of, rows * top, reach, slope, True), portions_of(number_of, rows * top, reach, slope, False)
    places = jnp.arange(number_of)

    def named(tallies, turn):
        used = int((tallies > 0).sum())
        fixed = max(1, used // 4)
        passed = fixed + (places - fixed + turn * (used - fixed)) % max(1, number_of - fixed)
        return jnp.zeros((number_of,), jnp.int32).at[order[jnp.where(places < fixed, places, passed)]].set(jnp.asarray(tallies, jnp.int32))

    tallies = jnp.where(number % 4 == 0, named(packed, number // 4), named(usual, number - number // 4 - 1))
    mixed = jax.random.permutation(jax.random.fold_in(own, 3), number_of)
    donor, receiver = mixed[0:number_of // 2 * 2:2], mixed[1:number_of // 2 * 2:2]
    slack = jnp.minimum(tallies[donor] - 1, reach - tallies[receiver]) // 2
    slack = jnp.where((donor == order[0]) | (receiver == order[0]) | (tallies[receiver] == 0), 0, jnp.maximum(slack, 0))
    passed = jax.random.randint(jax.random.fold_in(own, 4), (number_of // 2,), 0, 1 << 20) % (slack + 1)
    tallies = tallies.at[donor].add(-passed).at[receiver].add(passed)
    members = jnp.searchsorted(jnp.cumsum(tallies), jnp.arange(rows * top), side="right").astype(jnp.int32)
    grid = members.reshape(top, rows).T
    grid = grid[jax.random.permutation(jax.random.fold_in(own, 1), rows)]
    turn = jax.random.randint(jax.random.fold_in(own, 2), (rows, 1), 0, top)
    return jnp.take_along_axis(grid, (jnp.arange(top)[None, :] + turn) % top, axis=1)


def portions_of(number_of, total, reach, lean, full):
    loads = [(1 << 20) // math.isqrt(standing ** lean) + 1 for standing in range(1, number_of + 1)]
    largest = reach if full else min(reach, max(-(-total // number_of), total * loads[0] // sum(loads)))
    least = 1 if total - largest >= number_of - 1 else 0
    counts, rest = [largest] + [least] * (number_of - 1), total - largest - least * (number_of - 1)
    while rest > 0:
        candidates = [i for i in range(1, number_of) if counts[i] < largest] or [i for i in range(1, number_of) if counts[i] < reach]
        whole, remaining = sum([loads[i] for i in candidates]), rest
        for i in candidates:
            extra = min(reach - counts[i], max(1, remaining * loads[i] // whole), rest)
            counts[i] = counts[i] + extra
            rest = rest - extra
    return np.array(counts)


def noise(key, shape, deviation, bound, pieces=(), kind=jnp.bfloat16):
    factor_of = steps_of(key, shape, pieces, -0.22, 0.18) if pieces else 1.0
    drawn = jax.random.normal(key, shape, jnp.float32) * deviation * factor_of
    return jnp.minimum(jnp.maximum(drawn, -bound), bound).astype(kind)


def setup_inputs(seed: int = 0) -> dict:
    splits = jax.random.split(jax.random.key(seed), 14)
    tokens = noise(splits[0], (TOKENS, D), 1.0, 6.0, ((0, 32),))
    segments = draw_segments(jax.random.fold_in(splits[13], 71), 0)
    routes_keys = jax.random.split(jax.random.fold_in(splits[2], 1), TOKENS // TOK_DEV)
    routes_turns = jax.random.permutation(jax.random.fold_in(splits[2], 3), TOKENS // TOK_DEV)
    routes = jax.vmap(lambda own, number: assign_block(jax.random.fold_in(splits[2], 2), own, number, TOK_DEV, EXPERTS, 1, CAP, 1))(routes_keys, routes_turns).reshape((TOKENS, 1))
    buckets = place_ends(jax.random.randint(splits[3], (2 * LEN - 1,), 0, NB), jax.random.fold_in(splits[3], 1), 0, NB - 1).astype(jnp.int32)
    gain_attn = jnp.clip(1.0 + 0.1 * jax.random.normal(splits[4], (D,), jnp.float32), 0.5, 1.5)
    gain_moe = jnp.clip(1.0 + 0.1 * jax.random.normal(splits[5], (D,), jnp.float32), 0.5, 1.5)
    rel_table = noise(splits[6], (NB, H), 1.0, 6.0, (), jnp.float32)
    router_weight = noise(splits[7], (D, EXPERTS), 0.0185, 0.111, (), jnp.float32)
    qkv_weight = noise(splits[8], (D, 3 * D), D ** -0.5, 0.21875, ((0, 4),))
    out_weight = noise(splits[9], (D, D), (max(D // 256, 1)) ** -0.5, 3.5, ((0, 4),))
    w_in = noise(splits[10], (EXPERTS, D, FF), D ** -0.5, 0.21875, ((0, 8), (1, 4)))
    w_out = noise(splits[11], (EXPERTS, FF, D), (max(FF // (EXPERTS * EXPERTS), 1)) ** -0.5, 0.875, ((0, 8), (1, 4)))
    out_grad = noise(splits[12], (TOKENS, D), 1.0, 6.0, ((0, 32),))
    return dict(tokens=tokens, segments=segments, routes=routes, buckets=buckets, gain_attn=gain_attn, gain_moe=gain_moe, rel_table=rel_table, router_weight=router_weight, qkv_weight=qkv_weight, out_weight=out_weight, w_in=w_in, w_out=w_out, out_grad=out_grad)


epsilon = 1e-06
neg_large = -1000000000.0
highest = lax.Precision.HIGHEST

@jax.custom_vjp
def low(v):
    return lax.optimization_barrier(v.astype(jnp.bfloat16)).astype(jnp.float32)

@jax.custom_vjp
def low_back(v):
    return v

def low_keep(v):
    return (low(v), None)

def low_pass(kept, grad):
    return (grad,)

def back_keep(v):
    return (v, None)

def back_low(kept, grad):
    return (low(grad),)
low.defvjp(low_keep, low_pass)
low_back.defvjp(back_keep, back_low)

def rms_rows(values, gain):
    return values * lax.rsqrt(lax.optimization_barrier(jnp.mean(values * values, axis=-1, keepdims=True)) + epsilon) * gain

def attend_block(inputs, key_block, value_block, key_seg, offsets_t):
    query_block, query_at, query_seg = inputs
    scores = jnp.einsum('qhd,khd->hqk', query_block, key_block, precision=highest) * HD ** (-0.5)
    key_at = jnp.arange(LEN, dtype=jnp.int32)
    index_grid = key_at[None, :] - query_at[:, None] + (LEN - 1)
    scores = scores + jnp.take(offsets_t, index_grid, axis=1)
    scores = low_back(scores)
    allowed = query_seg[:, None] == key_seg[None, :]
    scores = jnp.where(allowed[None], scores, neg_large)
    weights = low(jax.nn.softmax(scores, axis=-1))
    return jnp.einsum('hqk,khd->qhd', weights, value_block, precision=highest)

def attend_sequence(items, offsets_t):
    query_seq, key_seq, value_seq, seg_seq = items
    block_rows = min(512, LEN)
    block_count = LEN // block_rows
    query_blocks = query_seq.reshape(block_count, block_rows, H, HD)
    place_blocks = jnp.arange(LEN, dtype=jnp.int32).reshape(block_count, block_rows)
    seg_blocks = seg_seq.reshape(block_count, block_rows)
    worker = jax.checkpoint(lambda inputs: attend_block(inputs, key_seq, value_seq, seg_seq, offsets_t))
    results = lax.map(worker, (query_blocks, place_blocks, seg_blocks))
    return results.reshape(LEN, H, HD)

def expert_apply(items):
    inputs_e, w_in_e, w_out_e = items
    pre = low_back(jnp.dot(inputs_e, w_in_e, precision=highest))
    hidden_ff = low(jax.nn.gelu(pre, approximate=False))
    return low(low_back(jnp.dot(hidden_ff, w_out_e, precision=highest)))

def reference(tokens, segments, routes, buckets, gain_attn, gain_moe, rel_table, router_weight, qkv_weight, out_weight, w_in, w_out, out_grad):
    block_total = TOKENS // TOK_DEV
    route_flat = routes[:, 0].astype(jnp.int32)
    onehot_int = (route_flat.reshape(block_total, TOK_DEV)[:, :, None] == jnp.arange(EXPERTS, dtype=jnp.int32)[None, None, :]).astype(jnp.int32)
    ranks = lax.optimization_barrier(jnp.sum((jnp.cumsum(onehot_int, axis=1) - 1) * onehot_int, axis=2)).reshape(-1).astype(jnp.int32)
    slot_of = jnp.arange(TOKENS, dtype=jnp.int32) // TOK_DEV * CAP + ranks
    slot_table = jnp.full((EXPERTS, block_total * CAP), TOKENS, dtype=jnp.int32)
    slot_table = slot_table.at[route_flat, slot_of].set(jnp.arange(TOKENS, dtype=jnp.int32))
    seg_seq = segments.reshape(SEQS, LEN)
    bucket_onehot = jax.nn.one_hot(buckets, NB, dtype=jnp.float32)

    def forward(inputs, gain_a, gain_m, table, router, qkv_w, out_w, w_in_f, w_out_f):
        offsets_t = jnp.dot(bucket_onehot, table, precision=highest).T
        normed_attn = low(rms_rows(inputs, gain_a))
        qkv = low(low_back(jnp.dot(normed_attn, qkv_w, precision=highest)))
        query_all = qkv[:, :D].reshape(SEQS, LEN, H, HD)
        key_all = qkv[:, D:2 * D].reshape(SEQS, LEN, H, HD)
        value_all = qkv[:, 2 * D:].reshape(SEQS, LEN, H, HD)
        sequence_fn = jax.checkpoint(lambda items: attend_sequence(items, offsets_t))
        attended = lax.map(sequence_fn, (query_all, key_all, value_all, seg_seq))
        attended = low(low_back(attended.reshape(TOKENS, D)))
        branch = low_back(jnp.dot(attended, out_w, precision=highest))
        hidden1 = inputs + branch
        normed_moe = rms_rows(hidden1, gain_m)
        logits = jnp.dot(normed_moe, router, precision=highest)
        router_probs = jax.nn.softmax(logits, axis=-1)
        gate = jnp.take_along_axis(router_probs, routes.astype(jnp.int32), axis=1)[:, 0]
        expert_in = low(low_back(normed_moe))
        padded = jnp.concatenate([expert_in, jnp.zeros((1, D), jnp.float32)], axis=0)
        gathered = padded[slot_table]
        slot_results = lax.map(jax.checkpoint(expert_apply), (gathered, w_in_f, w_out_f))
        expert_out = slot_results[route_flat, slot_of]
        return hidden1 + gate[:, None] * expert_out
    primals = (tokens.astype(jnp.float32), gain_attn, gain_moe, rel_table, router_weight, qkv_weight.astype(jnp.float32), out_weight.astype(jnp.float32), w_in.astype(jnp.float32), w_out.astype(jnp.float32))
    result, pullback = jax.vjp(forward, *primals)
    grads = pullback(out_grad.astype(jnp.float32))
    return (result.astype(jnp.bfloat16), grads[0], grads[1], grads[2], grads[3], grads[4], grads[5], grads[6], grads[7], grads[8])
```

```python
from functools import partial

import jax
import jax.numpy as jnp
from jax import lax
from jax.experimental import pallas as pl
from jax.experimental.pallas import tpu as pltpu
from jax.sharding import PartitionSpec as P

epsilon = 1e-06
neg_large = -1000000000.0
highest = lax.Precision.HIGHEST
tile_rows = 128
vmem_grant = 40 * 1024 * 1024


def norm_rows(values, gain):
    inverse = lax.rsqrt(jnp.mean(values * values, axis=1, keepdims=True) + epsilon)
    return (values * inverse * gain, inverse)


def norm_back(values, inverse, gain, upstream):
    scaled = upstream * gain
    gain_grad = jnp.sum(upstream * values * inverse, axis=0)
    input_grad = inverse * scaled - values * inverse**3 * jnp.mean(
        scaled * values, axis=1, keepdims=True
    )
    return (input_grad, gain_grad)


def contract_rows(left, right, precision_level=None):
    return lax.dot_general(
        left,
        right,
        (((0,), (0,)), ((), ())),
        precision=precision_level,
        preferred_element_type=jnp.float32,
    )


def toeplitz_rows(seed, rows):
    grid = seed
    while grid.shape[0] < rows:
        grid = jnp.concatenate([grid, pltpu.roll(grid, grid.shape[0], 1)], axis=0)
    return grid


def fold_rows(grid):
    width = grid.shape[1]
    while grid.shape[0] > 8:
        half = grid.shape[0] // 2
        grid = grid[:half] + pltpu.roll(grid[half:], width - half, 1)
    return grid


def dot_last(left, right):
    return lax.dot_general(
        left, right, (((1,), (1,)), ((), ())), preferred_element_type=jnp.float32
    )


def attend_kernel(scale, q_ref, k_ref, v_ref, seed_ref, segq_ref, segk_ref, out_ref, log_ref):
    rows, lanes = q_ref.shape
    keys = k_ref.shape[0]
    left_half = lax.broadcasted_iota(jnp.int32, (tile_rows, lanes), 1) < lanes // 2
    key_part, value_part = k_ref[...], v_ref[...]
    seg_k = segk_ref[...]
    zero = jnp.zeros((), jnp.bfloat16)
    grids = [toeplitz_rows(seed_ref[head], tile_rows) for head in range(2)]
    for first in range(0, rows, tile_rows):
        here = pl.ds(first, tile_rows)
        allowed = segq_ref[here, :] == seg_k
        query = q_ref[here, :] * scale
        found = []
        for head in range(2):
            own = left_half if head == 0 else ~left_half
            start = rows - first
            scores = dot_last(jnp.where(own, query, zero), key_part)
            scores = scores + grids[head][:, start : start + keys]
            scores = jnp.where(allowed, scores, neg_large)
            top = jnp.max(scores, axis=1, keepdims=True)
            weights = jnp.exp(scores - top)
            total = jnp.sum(weights, axis=1, keepdims=True)
            mixed = jnp.dot(
                weights.astype(jnp.bfloat16), value_part, preferred_element_type=jnp.float32
            )
            found.append((mixed / total, top + jnp.log(total)))
        out_ref[here, :] = jnp.where(left_half, found[0][0], found[1][0])
        log_ref[here, :] = jnp.where(left_half, found[0][1], found[1][1])


def attend_back_kernel(
    scale,
    q_ref,
    k_ref,
    v_ref,
    seed_ref,
    segq_ref,
    segk_ref,
    att_ref,
    log_ref,
    grad_ref,
    dq_ref,
    dkv_ref,
    dbias_ref,
    weight_scr,
    score_scr,
    query_scr,
    grad_scr,
):
    rows, lanes = q_ref.shape
    keys = k_ref.shape[0]
    left_half = lax.broadcasted_iota(jnp.int32, (tile_rows, lanes), 1) < lanes // 2
    key_part, value_part = k_ref[...], v_ref[...]
    seg_k = segk_ref[...]
    zero = jnp.zeros((), jnp.bfloat16)
    grids = [toeplitz_rows(seed_ref[head], tile_rows) for head in range(2)]
    sums = [None, None]
    for first in range(0, rows, tile_rows):
        here = pl.ds(first, tile_rows)
        allowed = segq_ref[here, :] == seg_k
        query = q_ref[here, :] * scale
        grad = grad_ref[here, :]
        product = grad.astype(jnp.float32) * att_ref[here, :]
        log_rows = log_ref[here, :]
        found = []
        for head in range(2):
            own = left_half if head == 0 else ~left_half
            start = rows - first
            put = pl.ds(head * rows + first, tile_rows)
            query_own = jnp.where(own, query, zero)
            grad_own = jnp.where(own, grad, zero)
            query_scr[put, :] = query_own
            grad_scr[put, :] = grad_own
            delta = jnp.sum(jnp.where(own, product, 0.0), axis=1, keepdims=True)
            lane = head * (lanes // 2)
            scores = dot_last(query_own, key_part) + grids[head][:, start : start + keys]
            weights = jnp.where(
                allowed, jnp.exp(scores - log_rows[:, lane : lane + 1]), 0.0
            )
            weight_grad = dot_last(grad_own, value_part)
            score_grad = (weights * (weight_grad - delta)).astype(jnp.bfloat16)
            weight_scr[put, :] = weights.astype(jnp.bfloat16)
            score_scr[put, :] = score_grad
            found.append(jnp.dot(score_grad, key_part, preferred_element_type=jnp.float32))
            pieces = [jnp.zeros((tile_rows, start), jnp.float32), score_grad.astype(jnp.float32)]
            if first > 0:
                pieces.append(jnp.zeros((tile_rows, first), jnp.float32))
            placed = jnp.concatenate(pieces, axis=1)
            sums[head] = placed if sums[head] is None else sums[head] + placed
        dq_ref[here, :] = (jnp.where(left_half, found[0], found[1]) * scale).astype(jnp.bfloat16)
    for head in range(2):
        dbias_ref[head] = fold_rows(sums[head])
    dkv_ref[:, :lanes] = contract_rows(score_scr[...], query_scr[...]).astype(jnp.bfloat16)
    dkv_ref[:, lanes:] = contract_rows(weight_scr[...], grad_scr[...]).astype(jnp.bfloat16)


def pair_specs(rows, keys, pairs, lanes, window):
    return [
        pl.BlockSpec((rows, lanes), lambda i: (0, i)),
        pl.BlockSpec((keys, lanes), lambda i: (0, i)),
        pl.BlockSpec((keys, lanes), lambda i: (0, pairs + i)),
        pl.BlockSpec((2, 8, window), lambda i: (i, 0, 0)),
        pl.BlockSpec((rows, 1), lambda i: (0, 0)),
        pl.BlockSpec((1, keys), lambda i: (0, 0)),
    ]


def attend(qkv_b, kv_all, seeds, seg_q, seg_k, head_size):
    rows, keys = qkv_b.shape[0], kv_all.shape[0]
    width, lanes = kv_all.shape[1] // 2, 2 * head_size
    pairs, window = width // lanes, seeds.shape[2]
    here = pl.BlockSpec((rows, lanes), lambda i: (0, i))
    return pl.pallas_call(
        partial(attend_kernel, head_size ** (-0.5)),
        grid=(pairs,),
        in_specs=pair_specs(rows, keys, pairs, lanes, window),
        out_specs=[here, here],
        out_shape=[jax.ShapeDtypeStruct((rows, width), jnp.float32)] * 2,
        compiler_params=pltpu.CompilerParams(vmem_limit_bytes=vmem_grant),
        cost_estimate=pl.CostEstimate(
            flops=8 * rows * keys * width,
            bytes_accessed=4 * keys * width + 10 * rows * width,
            transcendentals=2 * pairs * rows * keys,
        ),
    )(qkv_b, kv_all, kv_all, seeds, seg_q, seg_k)


def attend_back(qkv_b, kv_all, seeds, seg_q, seg_k, attended32, log_rows, grad_attended, head_size):
    rows, keys = qkv_b.shape[0], kv_all.shape[0]
    width, lanes = kv_all.shape[1] // 2, 2 * head_size
    pairs, window = width // lanes, seeds.shape[2]
    here = pl.BlockSpec((rows, lanes), lambda i: (0, i))
    return pl.pallas_call(
        partial(attend_back_kernel, head_size ** (-0.5)),
        grid=(pairs,),
        in_specs=pair_specs(rows, keys, pairs, lanes, window) + [here, here, here],
        out_specs=[
            here,
            pl.BlockSpec((keys, 2 * lanes), lambda i: (0, i)),
            pl.BlockSpec((2, 8, window), lambda i: (i, 0, 0)),
        ],
        out_shape=[
            jax.ShapeDtypeStruct((rows, width), jnp.bfloat16),
            jax.ShapeDtypeStruct((keys, 2 * width), jnp.bfloat16),
            jax.ShapeDtypeStruct(seeds.shape, jnp.float32),
        ],
        scratch_shapes=[
            pltpu.VMEM((2 * rows, keys), jnp.bfloat16),
            pltpu.VMEM((2 * rows, keys), jnp.bfloat16),
            pltpu.VMEM((2 * rows, lanes), jnp.bfloat16),
            pltpu.VMEM((2 * rows, lanes), jnp.bfloat16),
        ],
        compiler_params=pltpu.CompilerParams(vmem_limit_bytes=vmem_grant),
        cost_estimate=pl.CostEstimate(
            flops=20 * rows * keys * width,
            bytes_accessed=8 * keys * width + 14 * rows * width,
            transcendentals=2 * pairs * rows * keys,
        ),
    )(qkv_b, kv_all, kv_all, seeds, seg_q, seg_k, attended32, log_rows, grad_attended)


def body(
    tokens,
    segments,
    routes,
    buckets,
    gain_attn,
    gain_moe,
    rel_table,
    router_weight,
    qkv_weight,
    out_weight,
    w_in,
    w_out,
    out_grad,
):
    rows_here = tokens.shape[0]
    width = tokens.shape[1]
    heads = rel_table.shape[1]
    head_size = width // heads
    experts = router_weight.shape[1]
    capacity = 2 * rows_here // experts
    score_scale = head_size ** (-0.5)
    shard_count = lax.axis_size("shard")
    query_base = lax.axis_index("shard") * rows_here
    qkv_full, out_full = (
        lax.all_gather(qkv_weight, "shard", axis=0, tiled=True),
        lax.all_gather(out_weight, "shard", axis=0, tiled=True),
    )
    in_full, out_ff_full = (
        lax.all_gather(w_in[0], "shard", axis=0, tiled=True),
        lax.all_gather(w_out[0], "shard", axis=0, tiled=True),
    )
    inputs32 = tokens.astype(jnp.float32)
    normed_attn, inverse_attn = norm_rows(inputs32, gain_attn)
    normed_attn_b = normed_attn.astype(jnp.bfloat16)
    qkv_b = jnp.dot(normed_attn_b, qkv_full, preferred_element_type=jnp.float32).astype(
        jnp.bfloat16
    )
    key_value = qkv_b[:, width:]
    bucket_onehot = jax.nn.one_hot(buckets, rel_table.shape[0], dtype=jnp.float32)
    offsets_t = jnp.dot(
        bucket_onehot, rel_table, precision=highest, preferred_element_type=jnp.float32
    ).T
    length = shard_count * rows_here
    window = length + rows_here
    window_first = length - rows_here - query_base
    offsets_pad = jnp.concatenate([jnp.zeros((heads, 1), jnp.float32), offsets_t], axis=1)
    offsets_here = lax.dynamic_slice_in_dim(offsets_pad, window_first, window, 1)
    seeds = jnp.stack([jnp.roll(offsets_here, row, axis=1) for row in range(8)], axis=1)
    kv_all = lax.all_gather(key_value, "shard", axis=0, tiled=True)
    seg_k = lax.all_gather(segments, "shard", axis=0, tiled=True)[None, :]
    seg_q = segments[:, None]
    attended32, log_rows = attend(qkv_b, kv_all, seeds, seg_q, seg_k, head_size)
    attended_b = attended32.astype(jnp.bfloat16)
    hidden1 = inputs32 + jnp.dot(attended_b, out_full, preferred_element_type=jnp.float32)
    normed_moe, inverse_moe = norm_rows(hidden1, gain_moe)
    logits = jnp.dot(
        normed_moe, router_weight, precision=highest, preferred_element_type=jnp.float32
    )
    router_probs = jax.nn.softmax(logits, axis=1)
    route = routes[:, 0]
    route_onehot = (route[:, None] == jnp.arange(experts, dtype=jnp.int32)[None, :]).astype(
        jnp.float32
    )
    gate = jnp.sum(router_probs * route_onehot, axis=1)
    onehot_count = route_onehot.astype(jnp.int32)
    rank_in_expert = jnp.sum((jnp.cumsum(onehot_count, axis=0) - 1) * onehot_count, axis=1)
    slot_id = route * capacity + rank_in_expert
    dispatch = (
        jnp.arange(experts * capacity, dtype=jnp.int32)[:, None] == slot_id[None, :]
    ).astype(jnp.bfloat16)
    send_rows = jnp.dot(
        dispatch, normed_moe.astype(jnp.bfloat16), preferred_element_type=jnp.float32
    ).astype(jnp.bfloat16)
    send_rows = send_rows.reshape(experts, capacity, width)
    received = lax.all_to_all(send_rows, "expert", split_axis=0, concat_axis=0, tiled=True)
    sources = received.shape[0]
    item_count = received.shape[1]
    pre = jnp.dot(received.reshape(-1, width), in_full, preferred_element_type=jnp.float32)
    hidden_ff = jax.nn.gelu(pre, approximate=False).astype(jnp.bfloat16)
    result = jnp.dot(hidden_ff, out_ff_full, preferred_element_type=jnp.float32).astype(
        jnp.bfloat16
    )
    returned_rows = lax.all_to_all(
        result.reshape(sources, item_count, width),
        "expert",
        split_axis=0,
        concat_axis=0,
        tiled=True,
    )
    pre_kept = pre.reshape(sources, item_count, -1)
    expert_out = contract_rows(dispatch, returned_rows.reshape(-1, width))
    output = (hidden1 + gate[:, None] * expert_out).astype(jnp.bfloat16)
    upstream = out_grad.astype(jnp.float32)
    gate_grad = jnp.sum(upstream * expert_out, axis=1)
    grad_slots = jnp.dot(
        dispatch,
        (gate[:, None] * upstream).astype(jnp.bfloat16),
        preferred_element_type=jnp.float32,
    ).astype(jnp.bfloat16)
    grad_received = lax.all_to_all(
        grad_slots.reshape(experts, capacity, width),
        "expert",
        split_axis=0,
        concat_axis=0,
        tiled=True,
    )
    grad_flat = grad_received.reshape(-1, width)
    pre_flat = pre_kept.reshape(grad_flat.shape[0], -1)
    hidden_ff, gelu_back = jax.vjp(partial(jax.nn.gelu, approximate=False), pre_flat)
    hidden_b = hidden_ff.astype(jnp.bfloat16)
    grad_hidden = lax.dot_general(
        grad_flat, out_ff_full, (((1,), (1,)), ((), ())), preferred_element_type=jnp.float32
    )
    grad_pre = gelu_back(grad_hidden)[0].astype(jnp.bfloat16)
    grad_back_rows = lax.dot_general(
        grad_pre, in_full, (((1,), (1,)), ((), ())), preferred_element_type=jnp.float32
    ).astype(jnp.bfloat16)
    returned_grad = lax.all_to_all(
        grad_back_rows.reshape(grad_received.shape),
        "expert",
        split_axis=0,
        concat_axis=0,
        tiled=True,
    )
    grad_in_part = contract_rows(received.reshape(-1, width), grad_pre)
    grad_out_part = contract_rows(hidden_b, grad_flat)
    grad_in_rows, grad_out_rows = (
        lax.psum_scatter(
            grad_in_part.astype(jnp.bfloat16), "shard", scatter_dimension=0, tiled=True
        ).astype(jnp.float32),
        lax.psum_scatter(
            grad_out_part.astype(jnp.bfloat16), "shard", scatter_dimension=0, tiled=True
        ).astype(jnp.float32),
    )
    grad_expert_in = contract_rows(dispatch, returned_grad.reshape(-1, width))
    logit_grad = gate_grad[:, None] * router_probs * (route_onehot - gate[:, None])
    router_grad = contract_rows(normed_moe, logit_grad, highest)
    grad_normed_moe = grad_expert_in + lax.dot_general(
        logit_grad,
        router_weight,
        (((1,), (1,)), ((), ())),
        precision=highest,
        preferred_element_type=jnp.float32,
    )
    grad_moe_in, gain_moe_grad = norm_back(hidden1, inverse_moe, gain_moe, grad_normed_moe)
    grad_hidden1 = upstream + grad_moe_in
    branch_grad = grad_hidden1.astype(jnp.bfloat16)
    grad_attended = lax.dot_general(
        branch_grad, out_full, (((1,), (1,)), ((), ())), preferred_element_type=jnp.float32
    ).astype(jnp.bfloat16)
    query_grad, pair_grads, seed_grads = attend_back(
        qkv_b, kv_all, seeds, seg_q, seg_k, attended32, log_rows, grad_attended, head_size
    )
    kv_grad = lax.psum_scatter(pair_grads, "shard", scatter_dimension=0, tiled=True)
    kv_grad = kv_grad.reshape(rows_here, heads // 2, 2, 2 * head_size)
    kv_grad = kv_grad.transpose(0, 2, 1, 3).reshape(rows_here, 2 * width)
    grad_qkv_b = jnp.concatenate([query_grad, kv_grad], axis=1)
    grad_normed_attn = lax.dot_general(
        grad_qkv_b, qkv_full, (((1,), (1,)), ((), ())), preferred_element_type=jnp.float32
    )
    grad_attn_in, gain_attn_grad = norm_back(inputs32, inverse_attn, gain_attn, grad_normed_attn)
    grad_tokens = grad_hidden1 + grad_attn_in
    weight_rows = lax.psum_scatter(
        jnp.concatenate(
            [contract_rows(normed_attn_b, grad_qkv_b), contract_rows(attended_b, branch_grad)],
            axis=1,
        ).astype(jnp.bfloat16),
        "shard",
        scatter_dimension=0,
        tiled=True,
    ).astype(jnp.float32)
    weight_rows = lax.psum(weight_rows.astype(jnp.bfloat16), "expert").astype(jnp.float32)
    window_grad = sum(jnp.roll(seed_grads[:, row], -row, axis=1) for row in range(8))
    onehot_pad = jnp.concatenate([jnp.zeros_like(bucket_onehot[:1]), bucket_onehot], axis=0)
    onehot_here = lax.dynamic_slice_in_dim(onehot_pad, window_first, window, 0)
    table_grad = jnp.dot(
        window_grad, onehot_here, precision=highest, preferred_element_type=jnp.float32
    ).T
    gain_attn_total, gain_moe_total, table_total, router_total = lax.psum(
        (gain_attn_grad, gain_moe_grad, table_grad, router_grad), ("expert", "shard")
    )
    return (
        output,
        grad_tokens,
        gain_attn_total,
        gain_moe_total,
        table_total,
        router_total,
        weight_rows[:, : 3 * width],
        weight_rows[:, 3 * width :],
        grad_in_rows[None],
        grad_out_rows[None],
    )


def solution(mesh):
    in_specs = (
        P(("expert", "shard"), None),
        P(("expert", "shard")),
        P(("expert", "shard"), None),
        P(),
        P(),
        P(),
        P(),
        P(),
        P("shard", None),
        P("shard", None),
        P("expert", "shard", None),
        P("expert", "shard", None),
        P(("expert", "shard"), None),
    )
    out_specs = (
        P(("expert", "shard"), None),
        P(("expert", "shard"), None),
        P(),
        P(),
        P(),
        P(),
        P("shard", None),
        P("shard", None),
        P("expert", "shard", None),
        P("expert", "shard", None),
    )
    return jax.shard_map(body, mesh=mesh, in_specs=in_specs, out_specs=out_specs, check_vma=False)
```

```python
from functools import partial

import jax
import jax.numpy as jnp
from jax import lax
from jax.experimental import pallas as pl
from jax.experimental.pallas import tpu as pltpu
from jax.sharding import PartitionSpec as P

epsilon = 1e-06
neg_large = -1000000000.0
highest = lax.Precision.HIGHEST
tile_rows = 128
vmem_grant = 40 * 1024 * 1024


def norm_rows(values, gain):
    inverse = lax.rsqrt(jnp.mean(values * values, axis=1, keepdims=True) + epsilon)
    return (values * inverse * gain, inverse)


def norm_back(values, inverse, gain, upstream):
    scaled = upstream * gain
    gain_grad = jnp.sum(upstream * values * inverse, axis=0)
    input_grad = inverse * scaled - values * inverse**3 * jnp.mean(
        scaled * values, axis=1, keepdims=True
    )
    return (input_grad, gain_grad)


def contract_rows(left, right, precision_level=None):
    return lax.dot_general(
        left,
        right,
        (((0,), (0,)), ((), ())),
        precision=precision_level,
        preferred_element_type=jnp.float32,
    )


def toeplitz_rows(seed, rows):
    grid = seed
    while grid.shape[0] < rows:
        grid = jnp.concatenate([grid, pltpu.roll(grid, grid.shape[0], 1)], axis=0)
    return grid


def fold_rows(grid):
    width = grid.shape[1]
    while grid.shape[0] > 8:
        half = grid.shape[0] // 2
        grid = grid[:half] + pltpu.roll(grid[half:], width - half, 1)
    return grid


def dot_last(left, right):
    return lax.dot_general(
        left, right, (((1,), (1,)), ((), ())), preferred_element_type=jnp.float32
    )


def attend_kernel(scale, q_ref, k_ref, v_ref, seed_ref, segq_ref, segk_ref, out_ref, log_ref):
    rows, lanes = q_ref.shape
    keys = k_ref.shape[0]
    left_half = lax.broadcasted_iota(jnp.int32, (tile_rows, lanes), 1) < lanes // 2
    key_part, value_part = k_ref[...], v_ref[...]
    seg_k = segk_ref[...]
    zero = jnp.zeros((), jnp.bfloat16)
    grids = [toeplitz_rows(seed_ref[head], tile_rows) for head in range(2)]
    for first in range(0, rows, tile_rows):
        here = pl.ds(first, tile_rows)
        allowed = segq_ref[here, :] == seg_k
        query = q_ref[here, :] * scale
        found = []
        for head in range(2):
            own = left_half if head == 0 else ~left_half
            start = rows - first
            scores = dot_last(jnp.where(own, query, zero), key_part)
            scores = scores + grids[head][:, start : start + keys]
            scores = jnp.where(allowed, scores, neg_large)
            top = jnp.max(scores, axis=1, keepdims=True)
            weights = jnp.exp(scores - top)
            total = jnp.sum(weights, axis=1, keepdims=True)
            mixed = jnp.dot(
                weights.astype(jnp.bfloat16), value_part, preferred_element_type=jnp.float32
            )
            found.append((mixed / total, top + jnp.log(total)))
        out_ref[here, :] = jnp.where(left_half, found[0][0], found[1][0])
        log_ref[here, :] = jnp.where(left_half, found[0][1], found[1][1])


def attend_back_kernel(
    scale,
    q_ref,
    k_ref,
    v_ref,
    seed_ref,
    segq_ref,
    segk_ref,
    att_ref,
    log_ref,
    grad_ref,
    dq_ref,
    dkv_ref,
    dbias_ref,
    weight_scr,
    score_scr,
    query_scr,
    grad_scr,
):
    rows, lanes = q_ref.shape
    keys = k_ref.shape[0]
    left_half = lax.broadcasted_iota(jnp.int32, (tile_rows, lanes), 1) < lanes // 2
    key_part, value_part = k_ref[...], v_ref[...]
    seg_k = segk_ref[...]
    zero = jnp.zeros((), jnp.bfloat16)
    grids = [toeplitz_rows(seed_ref[head], tile_rows) for head in range(2)]
    sums = [None, None]
    for first in range(0, rows, tile_rows):
        here = pl.ds(first, tile_rows)
        allowed = segq_ref[here, :] == seg_k
        query = q_ref[here, :] * scale
        grad = grad_ref[here, :]
        product = grad.astype(jnp.float32) * att_ref[here, :]
        log_rows = log_ref[here, :]
        found = []
        for head in range(2):
            own = left_half if head == 0 else ~left_half
            start = rows - first
            put = pl.ds(head * rows + first, tile_rows)
            query_own = jnp.where(own, query, zero)
            grad_own = jnp.where(own, grad, zero)
            query_scr[put, :] = query_own
            grad_scr[put, :] = grad_own
            delta = jnp.sum(jnp.where(own, product, 0.0), axis=1, keepdims=True)
            lane = head * (lanes // 2)
            scores = dot_last(query_own, key_part) + grids[head][:, start : start + keys]
            weights = jnp.where(
                allowed, jnp.exp(scores - log_rows[:, lane : lane + 1]), 0.0
            )
            weight_grad = dot_last(grad_own, value_part)
            score_grad = (weights * (weight_grad - delta)).astype(jnp.bfloat16)
            weight_scr[put, :] = weights.astype(jnp.bfloat16)
            score_scr[put, :] = score_grad
            found.append(jnp.dot(score_grad, key_part, preferred_element_type=jnp.float32))
            pieces = [jnp.zeros((tile_rows, start), jnp.float32), score_grad.astype(jnp.float32)]
            if first > 0:
                pieces.append(jnp.zeros((tile_rows, first), jnp.float32))
            placed = jnp.concatenate(pieces, axis=1)
            sums[head] = placed if sums[head] is None else sums[head] + placed
        dq_ref[here, :] = (jnp.where(left_half, found[0], found[1]) * scale).astype(jnp.bfloat16)
    for head in range(2):
        dbias_ref[head] = fold_rows(sums[head])
    dkv_ref[:, :lanes] = contract_rows(score_scr[...], query_scr[...]).astype(jnp.bfloat16)
    dkv_ref[:, lanes:] = contract_rows(weight_scr[...], grad_scr[...]).astype(jnp.bfloat16)


def pair_specs(rows, keys, pairs, lanes, window):
    return [
        pl.BlockSpec((rows, lanes), lambda i: (0, i)),
        pl.BlockSpec((keys, lanes), lambda i: (0, i)),
        pl.BlockSpec((keys, lanes), lambda i: (0, pairs + i)),
        pl.BlockSpec((2, 8, window), lambda i: (i, 0, 0)),
        pl.BlockSpec((rows, 1), lambda i: (0, 0)),
        pl.BlockSpec((1, keys), lambda i: (0, 0)),
    ]


def attend(qkv_b, kv_all, seeds, seg_q, seg_k, head_size):
    rows, keys = qkv_b.shape[0], kv_all.shape[0]
    width, lanes = kv_all.shape[1] // 2, 2 * head_size
    pairs, window = width // lanes, seeds.shape[2]
    here = pl.BlockSpec((rows, lanes), lambda i: (0, i))
    return pl.pallas_call(
        partial(attend_kernel, head_size ** (-0.5)),
        grid=(pairs,),
        in_specs=pair_specs(rows, keys, pairs, lanes, window),
        out_specs=[here, here],
        out_shape=[jax.ShapeDtypeStruct((rows, width), jnp.float32)] * 2,
        compiler_params=pltpu.CompilerParams(vmem_limit_bytes=vmem_grant),
        cost_estimate=pl.CostEstimate(
            flops=8 * rows * keys * width,
            bytes_accessed=4 * keys * width + 10 * rows * width,
            transcendentals=2 * pairs * rows * keys,
        ),
    )(qkv_b, kv_all, kv_all, seeds, seg_q, seg_k)


def attend_back(qkv_b, kv_all, seeds, seg_q, seg_k, attended32, log_rows, grad_attended, head_size):
    rows, keys = qkv_b.shape[0], kv_all.shape[0]
    width, lanes = kv_all.shape[1] // 2, 2 * head_size
    pairs, window = width // lanes, seeds.shape[2]
    here = pl.BlockSpec((rows, lanes), lambda i: (0, i))
    return pl.pallas_call(
        partial(attend_back_kernel, head_size ** (-0.5)),
        grid=(pairs,),
        in_specs=pair_specs(rows, keys, pairs, lanes, window) + [here, here, here],
        out_specs=[
            here,
            pl.BlockSpec((keys, 2 * lanes), lambda i: (0, i)),
            pl.BlockSpec((2, 8, window), lambda i: (i, 0, 0)),
        ],
        out_shape=[
            jax.ShapeDtypeStruct((rows, width), jnp.bfloat16),
            jax.ShapeDtypeStruct((keys, 2 * width), jnp.bfloat16),
            jax.ShapeDtypeStruct(seeds.shape, jnp.float32),
        ],
        scratch_shapes=[
            pltpu.VMEM((2 * rows, keys), jnp.bfloat16),
            pltpu.VMEM((2 * rows, keys), jnp.bfloat16),
            pltpu.VMEM((2 * rows, lanes), jnp.bfloat16),
            pltpu.VMEM((2 * rows, lanes), jnp.bfloat16),
        ],
        compiler_params=pltpu.CompilerParams(vmem_limit_bytes=vmem_grant),
        cost_estimate=pl.CostEstimate(
            flops=20 * rows * keys * width,
            bytes_accessed=8 * keys * width + 14 * rows * width,
            transcendentals=2 * pairs * rows * keys,
        ),
    )(qkv_b, kv_all, kv_all, seeds, seg_q, seg_k, attended32, log_rows, grad_attended)


def swap(value, axis, mask):
    count = lax.axis_size(axis)
    return lax.ppermute(value, axis, [(place, place ^ mask) for place in range(count)])


def gather_parts(value, axis, unit, groups):
    mine = lax.axis_index(axis) // unit
    whole = jnp.zeros((groups,) + value.shape, value.dtype)
    whole = lax.dynamic_update_index_in_dim(whole, value, mine, 0)
    for step in range(1, groups):
        got = swap(value, axis, step * unit)
        whole = lax.dynamic_update_index_in_dim(whole, got, mine ^ step, 0)
    return whole.reshape((groups * value.shape[0],) + value.shape[1:])


def scatter_parts(value, axis, unit, groups):
    mine = lax.axis_index(axis) // unit
    parts = value.reshape((groups, value.shape[0] // groups) + value.shape[1:])
    total = lax.dynamic_index_in_dim(parts, mine, 0, False).astype(jnp.float32)
    for step in range(1, groups):
        piece = lax.dynamic_index_in_dim(parts, mine ^ step, 0, False)
        total = total + swap(piece, axis, step * unit).astype(jnp.float32)
    return total


def gather_rows(value, axis):
    count = lax.axis_size(axis)
    if count == 4:
        return gather_parts(value, axis, 1, count)
    return lax.all_gather(value, axis, axis=0, tiled=True)


def scatter_rows(value, axis):
    count = lax.axis_size(axis)
    if count == 4:
        return scatter_parts(value, axis, 1, count)
    return lax.psum_scatter(value, axis, scatter_dimension=0, tiled=True).astype(jnp.float32)


def sum_weights(value):
    core = lax.axis_index("expert") % 2 == 0
    stacks = lax.axis_size("expert") // 2
    half = value.shape[1] // 2
    left, right = value[:, :half], value[:, half:]
    mine, other = jnp.where(core, left, right), jnp.where(core, right, left)
    both = mine.astype(jnp.float32) + swap(other, "expert", 1).astype(jnp.float32)
    rows = scatter_rows(both.astype(jnp.bfloat16), "shard").astype(jnp.bfloat16)
    piece = scatter_parts(rows, "expert", 2, stacks).astype(jnp.bfloat16)
    rows = gather_parts(piece, "expert", 2, stacks)
    partner = swap(rows, "expert", 1)
    left, right = jnp.where(core, rows, partner), jnp.where(core, partner, rows)
    return jnp.concatenate([left, right], axis=1).astype(jnp.float32)


def body(
    tokens,
    segments,
    routes,
    buckets,
    gain_attn,
    gain_moe,
    rel_table,
    router_weight,
    qkv_weight,
    out_weight,
    w_in,
    w_out,
    out_grad,
):
    rows_here = tokens.shape[0]
    width = tokens.shape[1]
    heads = rel_table.shape[1]
    head_size = width // heads
    experts = router_weight.shape[1]
    capacity = 2 * rows_here // experts
    score_scale = head_size ** (-0.5)
    shard_count = lax.axis_size("shard")
    query_base = lax.axis_index("shard") * rows_here
    projections = lax.all_gather(
        jnp.concatenate([qkv_weight, out_weight], axis=1), "shard", axis=0, tiled=True
    )
    projections, own_in, own_out = lax.optimization_barrier((projections, w_in[0], w_out[0]))
    qkv_full, out_full = projections[:, : 3 * width], projections[:, 3 * width :]
    in_full = lax.all_gather(own_in, "shard", axis=0, tiled=True)
    out_ff_full = lax.all_gather(own_out, "shard", axis=0, tiled=True)
    inputs32 = tokens.astype(jnp.float32)
    normed_attn, inverse_attn = norm_rows(inputs32, gain_attn)
    normed_attn_b = normed_attn.astype(jnp.bfloat16)
    qkv_b = jnp.dot(normed_attn_b, qkv_full, preferred_element_type=jnp.float32).astype(
        jnp.bfloat16
    )
    key_value = qkv_b[:, width:]
    bucket_onehot = jax.nn.one_hot(buckets, rel_table.shape[0], dtype=jnp.float32)
    offsets_t = jnp.dot(
        bucket_onehot, rel_table, precision=highest, preferred_element_type=jnp.float32
    ).T
    length = shard_count * rows_here
    window = length + rows_here
    window_first = length - rows_here - query_base
    offsets_pad = jnp.concatenate([jnp.zeros((heads, 1), jnp.float32), offsets_t], axis=1)
    offsets_here = lax.dynamic_slice_in_dim(offsets_pad, window_first, window, 1)
    seeds = jnp.stack([jnp.roll(offsets_here, row, axis=1) for row in range(8)], axis=1)
    kv_all = gather_rows(key_value, "shard")
    seg_k = gather_rows(segments, "shard")[None, :]
    seg_q = segments[:, None]
    attended32, log_rows = attend(qkv_b, kv_all, seeds, seg_q, seg_k, head_size)
    attended_b = attended32.astype(jnp.bfloat16)
    hidden1 = inputs32 + jnp.dot(attended_b, out_full, preferred_element_type=jnp.float32)
    normed_moe, inverse_moe = norm_rows(hidden1, gain_moe)
    logits = jnp.dot(
        normed_moe, router_weight, precision=highest, preferred_element_type=jnp.float32
    )
    router_probs = jax.nn.softmax(logits, axis=1)
    route = routes[:, 0]
    route_onehot = (route[:, None] == jnp.arange(experts, dtype=jnp.int32)[None, :]).astype(
        jnp.float32
    )
    gate = jnp.sum(router_probs * route_onehot, axis=1)
    onehot_count = route_onehot.astype(jnp.int32)
    rank_in_expert = jnp.sum((jnp.cumsum(onehot_count, axis=0) - 1) * onehot_count, axis=1)
    slot_id = route * capacity + rank_in_expert
    dispatch = (
        jnp.arange(experts * capacity, dtype=jnp.int32)[:, None] == slot_id[None, :]
    ).astype(jnp.bfloat16)
    send_rows = jnp.dot(
        dispatch, normed_moe.astype(jnp.bfloat16), preferred_element_type=jnp.float32
    ).astype(jnp.bfloat16)
    send_rows = send_rows.reshape(experts, capacity, width)
    received = lax.all_to_all(send_rows, "expert", split_axis=0, concat_axis=0, tiled=True)
    sources = received.shape[0]
    item_count = received.shape[1]
    upstream = out_grad.astype(jnp.float32)
    grad_slots = jnp.dot(
        dispatch,
        (gate[:, None] * upstream).astype(jnp.bfloat16),
        preferred_element_type=jnp.float32,
    ).astype(jnp.bfloat16)
    grad_received = lax.all_to_all(
        grad_slots.reshape(experts, capacity, width),
        "expert",
        split_axis=0,
        concat_axis=0,
        tiled=True,
    )
    grad_flat = grad_received.reshape(-1, width)
    pre = jnp.dot(received.reshape(-1, width), in_full, preferred_element_type=jnp.float32)
    hidden_ff, gelu_back = jax.vjp(partial(jax.nn.gelu, approximate=False), pre)
    hidden_b = hidden_ff.astype(jnp.bfloat16)
    grad_out_part = contract_rows(hidden_b, grad_flat).astype(jnp.bfloat16)
    out_ff_full, grad_out_part = lax.optimization_barrier((out_ff_full, grad_out_part))
    grad_out_rows = lax.psum_scatter(grad_out_part, "shard", scatter_dimension=0, tiled=True)
    result = jnp.dot(hidden_b, out_ff_full, preferred_element_type=jnp.float32).astype(
        jnp.bfloat16
    )
    returned_rows = lax.all_to_all(
        result.reshape(sources, item_count, width),
        "expert",
        split_axis=0,
        concat_axis=0,
        tiled=True,
    )
    expert_out = contract_rows(dispatch, returned_rows.reshape(-1, width))
    output = (hidden1 + gate[:, None] * expert_out).astype(jnp.bfloat16)
    gate_grad = jnp.sum(upstream * expert_out, axis=1)
    grad_hidden = lax.dot_general(
        grad_flat, out_ff_full, (((1,), (1,)), ((), ())), preferred_element_type=jnp.float32
    )
    grad_pre = gelu_back(grad_hidden)[0].astype(jnp.bfloat16)
    grad_back_rows = lax.dot_general(
        grad_pre, in_full, (((1,), (1,)), ((), ())), preferred_element_type=jnp.float32
    ).astype(jnp.bfloat16)
    returned_grad = lax.all_to_all(
        grad_back_rows.reshape(grad_received.shape),
        "expert",
        split_axis=0,
        concat_axis=0,
        tiled=True,
    )
    grad_in_part = contract_rows(received.reshape(-1, width), grad_pre).astype(jnp.bfloat16)
    returned_grad, grad_in_part = lax.optimization_barrier((returned_grad, grad_in_part))
    grad_in_rows = lax.psum_scatter(grad_in_part, "shard", scatter_dimension=0, tiled=True)
    grad_expert_in = contract_rows(dispatch, returned_grad.reshape(-1, width))
    logit_grad = gate_grad[:, None] * router_probs * (route_onehot - gate[:, None])
    router_grad = contract_rows(normed_moe, logit_grad, highest)
    grad_normed_moe = grad_expert_in + lax.dot_general(
        logit_grad,
        router_weight,
        (((1,), (1,)), ((), ())),
        precision=highest,
        preferred_element_type=jnp.float32,
    )
    grad_moe_in, gain_moe_grad = norm_back(hidden1, inverse_moe, gain_moe, grad_normed_moe)
    grad_hidden1 = upstream + grad_moe_in
    branch_grad = grad_hidden1.astype(jnp.bfloat16)
    grad_attended = lax.dot_general(
        branch_grad, out_full, (((1,), (1,)), ((), ())), preferred_element_type=jnp.float32
    ).astype(jnp.bfloat16)
    grad_attended, grad_out_rows = lax.optimization_barrier((grad_attended, grad_out_rows))
    query_grad, pair_grads, seed_grads = attend_back(
        qkv_b, kv_all, seeds, seg_q, seg_k, attended32, log_rows, grad_attended, head_size
    )
    kv_grad = scatter_rows(pair_grads, "shard").astype(jnp.bfloat16)
    kv_grad = kv_grad.reshape(rows_here, heads // 2, 2, 2 * head_size)
    kv_grad = kv_grad.transpose(0, 2, 1, 3).reshape(rows_here, 2 * width)
    grad_qkv_b = jnp.concatenate([query_grad, kv_grad], axis=1)
    grad_normed_attn = lax.dot_general(
        grad_qkv_b, qkv_full, (((1,), (1,)), ((), ())), preferred_element_type=jnp.float32
    )
    grad_attn_in, gain_attn_grad = norm_back(inputs32, inverse_attn, gain_attn, grad_normed_attn)
    grad_tokens = grad_hidden1 + grad_attn_in
    weight_part = jnp.concatenate(
        [contract_rows(normed_attn_b, grad_qkv_b), contract_rows(attended_b, branch_grad)], axis=1
    ).astype(jnp.bfloat16)
    weight_part, grad_in_rows = lax.optimization_barrier((weight_part, grad_in_rows))
    weight_rows = sum_weights(weight_part)
    window_grad = sum(jnp.roll(seed_grads[:, row], -row, axis=1) for row in range(8))
    onehot_pad = jnp.concatenate([jnp.zeros_like(bucket_onehot[:1]), bucket_onehot], axis=0)
    onehot_here = lax.dynamic_slice_in_dim(onehot_pad, window_first, window, 0)
    table_grad = jnp.dot(
        window_grad, onehot_here, precision=highest, preferred_element_type=jnp.float32
    ).T
    gain_attn_total, gain_moe_total, table_total, router_total = lax.psum(
        (gain_attn_grad, gain_moe_grad, table_grad, router_grad), ("expert", "shard")
    )
    return (
        output,
        grad_tokens,
        gain_attn_total,
        gain_moe_total,
        table_total,
        router_total,
        weight_rows[:, : 3 * width],
        weight_rows[:, 3 * width :],
        grad_in_rows.astype(jnp.float32)[None],
        grad_out_rows.astype(jnp.float32)[None],
    )


def solution(mesh):
    in_specs = (
        P(("expert", "shard"), None),
        P(("expert", "shard")),
        P(("expert", "shard"), None),
        P(),
        P(),
        P(),
        P(),
        P(),
        P("shard", None),
        P("shard", None),
        P("expert", "shard", None),
        P("expert", "shard", None),
        P(("expert", "shard"), None),
    )
    out_specs = (
        P(("expert", "shard"), None),
        P(("expert", "shard"), None),
        P(),
        P(),
        P(),
        P(),
        P("shard", None),
        P("shard", None),
        P("expert", "shard", None),
        P("expert", "shard", None),
    )
    return jax.shard_map(body, mesh=mesh, in_specs=in_specs, out_specs=out_specs, check_vma=False)
```

```python
from functools import partial

import jax
import jax.numpy as jnp
from jax import lax
from jax.experimental import pallas as pl
from jax.experimental.pallas import tpu as pltpu
from jax.sharding import PartitionSpec as P

epsilon = 1e-06
neg_large = -1000000000.0
highest = lax.Precision.HIGHEST
tile_rows = 128
vmem_grant = 40 * 1024 * 1024


def norm_rows(values, gain):
    inverse = lax.rsqrt(jnp.mean(values * values, axis=1, keepdims=True) + epsilon)
    return (values * inverse * gain, inverse)


def norm_back(values, inverse, gain, upstream):
    scaled = upstream * gain
    gain_grad = jnp.sum(upstream * values * inverse, axis=0)
    input_grad = inverse * scaled - values * inverse**3 * jnp.mean(
        scaled * values, axis=1, keepdims=True
    )
    return (input_grad, gain_grad)


def contract_rows(left, right, precision_level=None):
    return lax.dot_general(
        left,
        right,
        (((0,), (0,)), ((), ())),
        precision=precision_level,
        preferred_element_type=jnp.float32,
    )


def toeplitz_rows(seed, rows):
    grid = seed
    while grid.shape[0] < rows:
        grid = jnp.concatenate([grid, pltpu.roll(grid, grid.shape[0], 1)], axis=0)
    return grid


def fold_rows(grid):
    width = grid.shape[1]
    while grid.shape[0] > 8:
        half = grid.shape[0] // 2
        grid = grid[:half] + pltpu.roll(grid[half:], width - half, 1)
    return grid


def dot_last(left, right):
    return lax.dot_general(
        left, right, (((1,), (1,)), ((), ())), preferred_element_type=jnp.float32
    )


def attend_kernel(scale, q_ref, k_ref, v_ref, seed_ref, segq_ref, segk_ref, out_ref, log_ref):
    rows, lanes = q_ref.shape
    keys = k_ref.shape[0]
    left_half = lax.broadcasted_iota(jnp.int32, (tile_rows, lanes), 1) < lanes // 2
    key_part, value_part = k_ref[...], v_ref[...]
    seg_k = segk_ref[...]
    zero = jnp.zeros((), jnp.bfloat16)
    grids = [toeplitz_rows(seed_ref[head], tile_rows) for head in range(2)]
    for first in range(0, rows, tile_rows):
        here = pl.ds(first, tile_rows)
        allowed = segq_ref[here, :] == seg_k
        query = q_ref[here, :] * scale
        found = []
        for head in range(2):
            own = left_half if head == 0 else ~left_half
            start = rows - first
            scores = dot_last(jnp.where(own, query, zero), key_part)
            scores = scores + grids[head][:, start : start + keys]
            scores = jnp.where(allowed, scores, neg_large)
            top = jnp.max(scores, axis=1, keepdims=True)
            weights = jnp.exp(scores - top)
            total = jnp.sum(weights, axis=1, keepdims=True)
            mixed = jnp.dot(
                weights.astype(jnp.bfloat16), value_part, preferred_element_type=jnp.float32
            )
            found.append((mixed / total, top + jnp.log(total)))
        out_ref[here, :] = jnp.where(left_half, found[0][0], found[1][0])
        log_ref[here, :] = jnp.where(left_half, found[0][1], found[1][1])


def attend_back_kernel(
    scale,
    q_ref,
    k_ref,
    v_ref,
    seed_ref,
    segq_ref,
    segk_ref,
    att_ref,
    log_ref,
    grad_ref,
    dq_ref,
    dkv_ref,
    dbias_ref,
    weight_scr,
    score_scr,
    query_scr,
    grad_scr,
):
    rows, lanes = q_ref.shape
    keys = k_ref.shape[0]
    left_half = lax.broadcasted_iota(jnp.int32, (tile_rows, lanes), 1) < lanes // 2
    key_part, value_part = k_ref[...], v_ref[...]
    seg_k = segk_ref[...]
    zero = jnp.zeros((), jnp.bfloat16)
    grids = [toeplitz_rows(seed_ref[head], tile_rows) for head in range(2)]
    sums = [None, None]
    for first in range(0, rows, tile_rows):
        here = pl.ds(first, tile_rows)
        allowed = segq_ref[here, :] == seg_k
        query = q_ref[here, :] * scale
        grad = grad_ref[here, :]
        product = grad.astype(jnp.float32) * att_ref[here, :]
        log_rows = log_ref[here, :]
        found = []
        for head in range(2):
            own = left_half if head == 0 else ~left_half
            start = rows - first
            put = pl.ds(head * rows + first, tile_rows)
            query_own = jnp.where(own, query, zero)
            grad_own = jnp.where(own, grad, zero)
            query_scr[put, :] = query_own
            grad_scr[put, :] = grad_own
            delta = jnp.sum(jnp.where(own, product, 0.0), axis=1, keepdims=True)
            lane = head * (lanes // 2)
            scores = dot_last(query_own, key_part) + grids[head][:, start : start + keys]
            weights = jnp.where(
                allowed, jnp.exp(scores - log_rows[:, lane : lane + 1]), 0.0
            )
            weight_grad = dot_last(grad_own, value_part)
            score_grad = (weights * (weight_grad - delta)).astype(jnp.bfloat16)
            weight_scr[put, :] = weights.astype(jnp.bfloat16)
            score_scr[put, :] = score_grad
            found.append(jnp.dot(score_grad, key_part, preferred_element_type=jnp.float32))
            pieces = [jnp.zeros((tile_rows, start), jnp.float32), score_grad.astype(jnp.float32)]
            if first > 0:
                pieces.append(jnp.zeros((tile_rows, first), jnp.float32))
            placed = jnp.concatenate(pieces, axis=1)
            sums[head] = placed if sums[head] is None else sums[head] + placed
        dq_ref[here, :] = (jnp.where(left_half, found[0], found[1]) * scale).astype(jnp.bfloat16)
    for head in range(2):
        dbias_ref[head] = fold_rows(sums[head])
    dkv_ref[:, :lanes] = contract_rows(score_scr[...], query_scr[...]).astype(jnp.bfloat16)
    dkv_ref[:, lanes:] = contract_rows(weight_scr[...], grad_scr[...]).astype(jnp.bfloat16)


def pair_specs(rows, keys, pairs, lanes, window):
    return [
        pl.BlockSpec((rows, lanes), lambda i: (0, i)),
        pl.BlockSpec((keys, lanes), lambda i: (0, i)),
        pl.BlockSpec((keys, lanes), lambda i: (0, pairs + i)),
        pl.BlockSpec((2, 8, window), lambda i: (i, 0, 0)),
        pl.BlockSpec((rows, 1), lambda i: (0, 0)),
        pl.BlockSpec((1, keys), lambda i: (0, 0)),
    ]


def attend(qkv_b, kv_all, seeds, seg_q, seg_k, head_size):
    rows, keys = qkv_b.shape[0], kv_all.shape[0]
    width, lanes = kv_all.shape[1] // 2, 2 * head_size
    pairs, window = width // lanes, seeds.shape[2]
    here = pl.BlockSpec((rows, lanes), lambda i: (0, i))
    return pl.pallas_call(
        partial(attend_kernel, head_size ** (-0.5)),
        grid=(pairs,),
        in_specs=pair_specs(rows, keys, pairs, lanes, window),
        out_specs=[here, here],
        out_shape=[jax.ShapeDtypeStruct((rows, width), jnp.float32)] * 2,
        compiler_params=pltpu.CompilerParams(vmem_limit_bytes=vmem_grant),
        cost_estimate=pl.CostEstimate(
            flops=8 * rows * keys * width,
            bytes_accessed=4 * keys * width + 10 * rows * width,
            transcendentals=2 * pairs * rows * keys,
        ),
    )(qkv_b, kv_all, kv_all, seeds, seg_q, seg_k)


def attend_back(qkv_b, kv_all, seeds, seg_q, seg_k, attended32, log_rows, grad_attended, head_size):
    rows, keys = qkv_b.shape[0], kv_all.shape[0]
    width, lanes = kv_all.shape[1] // 2, 2 * head_size
    pairs, window = width // lanes, seeds.shape[2]
    here = pl.BlockSpec((rows, lanes), lambda i: (0, i))
    return pl.pallas_call(
        partial(attend_back_kernel, head_size ** (-0.5)),
        grid=(pairs,),
        in_specs=pair_specs(rows, keys, pairs, lanes, window) + [here, here, here],
        out_specs=[
            here,
            pl.BlockSpec((keys, 2 * lanes), lambda i: (0, i)),
            pl.BlockSpec((2, 8, window), lambda i: (i, 0, 0)),
        ],
        out_shape=[
            jax.ShapeDtypeStruct((rows, width), jnp.bfloat16),
            jax.ShapeDtypeStruct((keys, 2 * width), jnp.bfloat16),
            jax.ShapeDtypeStruct(seeds.shape, jnp.float32),
        ],
        scratch_shapes=[
            pltpu.VMEM((2 * rows, keys), jnp.bfloat16),
            pltpu.VMEM((2 * rows, keys), jnp.bfloat16),
            pltpu.VMEM((2 * rows, lanes), jnp.bfloat16),
            pltpu.VMEM((2 * rows, lanes), jnp.bfloat16),
        ],
        compiler_params=pltpu.CompilerParams(vmem_limit_bytes=vmem_grant),
        cost_estimate=pl.CostEstimate(
            flops=20 * rows * keys * width,
            bytes_accessed=8 * keys * width + 14 * rows * width,
            transcendentals=2 * pairs * rows * keys,
        ),
    )(qkv_b, kv_all, kv_all, seeds, seg_q, seg_k, attended32, log_rows, grad_attended)


def swap(value, axis, mask):
    count = lax.axis_size(axis)
    return lax.ppermute(value, axis, [(place, place ^ mask) for place in range(count)])


def gather_parts(value, axis, unit, groups):
    mine = lax.axis_index(axis) // unit
    whole = jnp.zeros((groups,) + value.shape, value.dtype)
    whole = lax.dynamic_update_index_in_dim(whole, value, mine, 0)
    for step in range(1, groups):
        got = swap(value, axis, step * unit)
        whole = lax.dynamic_update_index_in_dim(whole, got, mine ^ step, 0)
    return whole.reshape((groups * value.shape[0],) + value.shape[1:])


def scatter_parts(value, axis, unit, groups):
    mine = lax.axis_index(axis) // unit
    parts = value.reshape((groups, value.shape[0] // groups) + value.shape[1:])
    total = lax.dynamic_index_in_dim(parts, mine, 0, False).astype(jnp.float32)
    for step in range(1, groups):
        piece = lax.dynamic_index_in_dim(parts, mine ^ step, 0, False)
        total = total + swap(piece, axis, step * unit).astype(jnp.float32)
    return total


def gather_rows(value, axis):
    count = lax.axis_size(axis)
    if count == 4:
        return gather_parts(value, axis, 1, count)
    return lax.all_gather(value, axis, axis=0, tiled=True)


def scatter_rows(value, axis):
    count = lax.axis_size(axis)
    if count == 4:
        return scatter_parts(value, axis, 1, count)
    return lax.psum_scatter(value, axis, scatter_dimension=0, tiled=True).astype(jnp.float32)


def gather_halves(value):
    core = lax.axis_index("expert") % 2 == 0
    half = value.shape[1] // 2
    mine = gather_rows(jnp.where(core, value[:, :half], value[:, half:]), "shard")
    partner = swap(mine, "expert", 1)
    left, right = jnp.where(core, mine, partner), jnp.where(core, partner, mine)
    return jnp.concatenate([left, right], axis=1)


def sum_weights(value):
    core = lax.axis_index("expert") % 2 == 0
    stacks = lax.axis_size("expert") // 2
    half = value.shape[1] // 2
    left, right = value[:, :half], value[:, half:]
    mine, other = jnp.where(core, left, right), jnp.where(core, right, left)
    both = mine.astype(jnp.float32) + swap(other, "expert", 1).astype(jnp.float32)
    rows = scatter_rows(both.astype(jnp.bfloat16), "shard").astype(jnp.bfloat16)
    piece = scatter_parts(rows, "expert", 2, stacks).astype(jnp.bfloat16)
    rows = gather_parts(piece, "expert", 2, stacks)
    partner = swap(rows, "expert", 1)
    left, right = jnp.where(core, rows, partner), jnp.where(core, partner, rows)
    return jnp.concatenate([left, right], axis=1).astype(jnp.float32)


def body(
    tokens,
    segments,
    routes,
    buckets,
    gain_attn,
    gain_moe,
    rel_table,
    router_weight,
    qkv_weight,
    out_weight,
    w_in,
    w_out,
    out_grad,
):
    rows_here = tokens.shape[0]
    width = tokens.shape[1]
    heads = rel_table.shape[1]
    head_size = width // heads
    experts = router_weight.shape[1]
    capacity = 2 * rows_here // experts
    score_scale = head_size ** (-0.5)
    shard_count = lax.axis_size("shard")
    query_base = lax.axis_index("shard") * rows_here
    projections = gather_halves(jnp.concatenate([qkv_weight, out_weight], axis=1))
    projections, own_in, own_out = lax.optimization_barrier((projections, w_in[0], w_out[0]))
    qkv_full, out_full = projections[:, : 3 * width], projections[:, 3 * width :]
    in_full = lax.all_gather(own_in, "shard", axis=0, tiled=True)
    out_ff_full = lax.all_gather(own_out, "shard", axis=0, tiled=True)
    inputs32 = tokens.astype(jnp.float32)
    normed_attn, inverse_attn = norm_rows(inputs32, gain_attn)
    normed_attn_b = normed_attn.astype(jnp.bfloat16)
    qkv_b = jnp.dot(normed_attn_b, qkv_full, preferred_element_type=jnp.float32).astype(
        jnp.bfloat16
    )
    key_value = qkv_b[:, width:]
    bucket_onehot = jax.nn.one_hot(buckets, rel_table.shape[0], dtype=jnp.float32)
    offsets_t = jnp.dot(
        bucket_onehot, rel_table, precision=highest, preferred_element_type=jnp.float32
    ).T
    length = shard_count * rows_here
    window = length + rows_here
    window_first = length - rows_here - query_base
    offsets_pad = jnp.concatenate([jnp.zeros((heads, 1), jnp.float32), offsets_t], axis=1)
    offsets_here = lax.dynamic_slice_in_dim(offsets_pad, window_first, window, 1)
    seeds = jnp.stack([jnp.roll(offsets_here, row, axis=1) for row in range(8)], axis=1)
    kv_all = gather_rows(key_value, "shard")
    seg_k = gather_rows(segments, "shard")[None, :]
    seg_q = segments[:, None]
    attended32, log_rows = attend(qkv_b, kv_all, seeds, seg_q, seg_k, head_size)
    attended_b = attended32.astype(jnp.bfloat16)
    hidden1 = inputs32 + jnp.dot(attended_b, out_full, preferred_element_type=jnp.float32)
    normed_moe, inverse_moe = norm_rows(hidden1, gain_moe)
    logits = jnp.dot(
        normed_moe, router_weight, precision=highest, preferred_element_type=jnp.float32
    )
    router_probs = jax.nn.softmax(logits, axis=1)
    route = routes[:, 0]
    route_onehot = (route[:, None] == jnp.arange(experts, dtype=jnp.int32)[None, :]).astype(
        jnp.float32
    )
    gate = jnp.sum(router_probs * route_onehot, axis=1)
    onehot_count = route_onehot.astype(jnp.int32)
    rank_in_expert = jnp.sum((jnp.cumsum(onehot_count, axis=0) - 1) * onehot_count, axis=1)
    slot_id = route * capacity + rank_in_expert
    dispatch = (
        jnp.arange(experts * capacity, dtype=jnp.int32)[:, None] == slot_id[None, :]
    ).astype(jnp.bfloat16)
    send_rows = jnp.dot(
        dispatch, normed_moe.astype(jnp.bfloat16), preferred_element_type=jnp.float32
    ).astype(jnp.bfloat16)
    send_rows = send_rows.reshape(experts, capacity, width)
    received = lax.all_to_all(send_rows, "expert", split_axis=0, concat_axis=0, tiled=True)
    sources = received.shape[0]
    item_count = received.shape[1]
    upstream = out_grad.astype(jnp.float32)
    grad_slots = jnp.dot(
        dispatch,
        (gate[:, None] * upstream).astype(jnp.bfloat16),
        preferred_element_type=jnp.float32,
    ).astype(jnp.bfloat16)
    grad_received = lax.all_to_all(
        grad_slots.reshape(experts, capacity, width),
        "expert",
        split_axis=0,
        concat_axis=0,
        tiled=True,
    )
    grad_flat = grad_received.reshape(-1, width)
    pre = jnp.dot(received.reshape(-1, width), in_full, preferred_element_type=jnp.float32)
    hidden_ff, gelu_back = jax.vjp(partial(jax.nn.gelu, approximate=False), pre)
    hidden_b = hidden_ff.astype(jnp.bfloat16)
    grad_out_part = contract_rows(hidden_b, grad_flat).astype(jnp.bfloat16)
    out_ff_full, grad_out_part = lax.optimization_barrier((out_ff_full, grad_out_part))
    grad_out_rows = lax.psum_scatter(grad_out_part, "shard", scatter_dimension=0, tiled=True)
    result = jnp.dot(hidden_b, out_ff_full, preferred_element_type=jnp.float32).astype(
        jnp.bfloat16
    )
    returned_rows = lax.all_to_all(
        result.reshape(sources, item_count, width),
        "expert",
        split_axis=0,
        concat_axis=0,
        tiled=True,
    )
    expert_out = contract_rows(dispatch, returned_rows.reshape(-1, width))
    output = (hidden1 + gate[:, None] * expert_out).astype(jnp.bfloat16)
    gate_grad = jnp.sum(upstream * expert_out, axis=1)
    grad_hidden = lax.dot_general(
        grad_flat, out_ff_full, (((1,), (1,)), ((), ())), preferred_element_type=jnp.float32
    )
    grad_pre = gelu_back(grad_hidden)[0].astype(jnp.bfloat16)
    grad_back_rows = lax.dot_general(
        grad_pre, in_full, (((1,), (1,)), ((), ())), preferred_element_type=jnp.float32
    ).astype(jnp.bfloat16)
    grad_back_rows, returned_rows = lax.optimization_barrier((grad_back_rows, returned_rows))
    returned_grad = lax.all_to_all(
        grad_back_rows.reshape(grad_received.shape),
        "expert",
        split_axis=0,
        concat_axis=0,
        tiled=True,
    )
    grad_in_part = contract_rows(received.reshape(-1, width), grad_pre).astype(jnp.bfloat16)
    returned_grad, grad_in_part = lax.optimization_barrier((returned_grad, grad_in_part))
    grad_in_rows = lax.psum_scatter(grad_in_part, "shard", scatter_dimension=0, tiled=True)
    grad_expert_in = contract_rows(dispatch, returned_grad.reshape(-1, width))
    logit_grad = gate_grad[:, None] * router_probs * (route_onehot - gate[:, None])
    router_grad = contract_rows(logit_grad, normed_moe, highest)
    grad_normed_moe = grad_expert_in + lax.dot_general(
        logit_grad,
        router_weight,
        (((1,), (1,)), ((), ())),
        precision=highest,
        preferred_element_type=jnp.float32,
    )
    grad_moe_in, gain_moe_grad = norm_back(hidden1, inverse_moe, gain_moe, grad_normed_moe)
    grad_hidden1 = upstream + grad_moe_in
    branch_grad = grad_hidden1.astype(jnp.bfloat16)
    grad_attended = lax.dot_general(
        branch_grad, out_full, (((1,), (1,)), ((), ())), preferred_element_type=jnp.float32
    ).astype(jnp.bfloat16)
    grad_attended, grad_out_rows = lax.optimization_barrier((grad_attended, grad_out_rows))
    query_grad, pair_grads, seed_grads = attend_back(
        qkv_b, kv_all, seeds, seg_q, seg_k, attended32, log_rows, grad_attended, head_size
    )
    kv_grad = scatter_rows(pair_grads, "shard").astype(jnp.bfloat16)
    kv_grad = kv_grad.reshape(rows_here, heads // 2, 2, 2 * head_size)
    kv_grad = kv_grad.transpose(0, 2, 1, 3).reshape(rows_here, 2 * width)
    grad_qkv_b = jnp.concatenate([query_grad, kv_grad], axis=1)
    grad_normed_attn = lax.dot_general(
        grad_qkv_b, qkv_full, (((1,), (1,)), ((), ())), preferred_element_type=jnp.float32
    )
    grad_attn_in, gain_attn_grad = norm_back(inputs32, inverse_attn, gain_attn, grad_normed_attn)
    grad_tokens = grad_hidden1 + grad_attn_in
    weight_part = jnp.concatenate(
        [contract_rows(normed_attn_b, grad_qkv_b), contract_rows(attended_b, branch_grad)], axis=1
    ).astype(jnp.bfloat16)
    weight_part, grad_in_rows = lax.optimization_barrier((weight_part, grad_in_rows))
    weight_rows = sum_weights(weight_part)
    window_grad = sum(jnp.roll(seed_grads[:, row], -row, axis=1) for row in range(8))
    onehot_pad = jnp.concatenate([jnp.zeros_like(bucket_onehot[:1]), bucket_onehot], axis=0)
    onehot_here = lax.dynamic_slice_in_dim(onehot_pad, window_first, window, 0)
    table_grad = jnp.dot(
        onehot_here.T, window_grad.T, precision=highest, preferred_element_type=jnp.float32
    )
    table_row = jnp.pad(table_grad.reshape(1, -1), ((0, 0), (0, width - table_grad.size)))
    small = jnp.concatenate(
        [gain_attn_grad[None], gain_moe_grad[None], table_row, router_grad], axis=0
    )
    totals = jnp.sum(lax.all_gather(small, ("expert", "shard")), axis=0)
    gain_attn_total, gain_moe_total = totals[0], totals[1]
    table_total = totals[2, : table_grad.size].reshape(table_grad.shape)
    router_total = totals[3:].T
    return (
        output,
        grad_tokens,
        gain_attn_total,
        gain_moe_total,
        table_total,
        router_total,
        weight_rows[:, : 3 * width],
        weight_rows[:, 3 * width :],
        grad_in_rows.astype(jnp.float32)[None],
        grad_out_rows.astype(jnp.float32)[None],
    )


def solution(mesh):
    in_specs = (
        P(("expert", "shard"), None),
        P(("expert", "shard")),
        P(("expert", "shard"), None),
        P(),
        P(),
        P(),
        P(),
        P(),
        P("shard", None),
        P("shard", None),
        P("expert", "shard", None),
        P("expert", "shard", None),
        P(("expert", "shard"), None),
    )
    out_specs = (
        P(("expert", "shard"), None),
        P(("expert", "shard"), None),
        P(),
        P(),
        P(),
        P(),
        P("shard", None),
        P("shard", None),
        P("expert", "shard", None),
        P("expert", "shard", None),
    )
    return jax.shard_map(body, mesh=mesh, in_specs=in_specs, out_specs=out_specs, check_vma=False)
```
